512 devices in a mesh: ctx: 64 (over z, x, core), hd: 8 (over y).
Axes of the slice: x: 4, y: 8, z: 8, core: 2. Of those that a mesh axis runs over, the one named last changes fastest.
Arguments:
- query_rows: bfloat16 [16384, 4096], P('ctx', 'hd'), may hold values from -240 to 240
- key_rows: bfloat16 [16384, 1024], P('ctx', 'hd'), may hold values from -3.5 to 3.5
- value_rows: bfloat16 [16384, 1024], P('ctx', 'hd'), may hold values from -6 to 6
- doc_ids: int32 [256], P('ctx'), may hold values from 0 to 17, never falling along the last dimension, each value on 1 to 160 neighbouring positions
- out_weight: bfloat16 [4096, 4096], P('hd'), may hold values from -0.125 to 0.125
Outputs:
- attended: bfloat16 [16384, 4096], P('ctx', 'hd')
- projected: bfloat16 [16384, 4096], P('ctx', 'hd')
The draws below stay inside these ranges and needn't reach their ends.
Inputs may be any that keep to these rules, and one draw needn't show every extreme that they name: `doc_ids`: ids never fall along the stretch; each of the 18 documents spans 1 to 160 whole blocks, and one spans exactly 160.
All inputs are finite; a program needn't handle non-finite values.
Results may differ from the reference program's by a relative error of at most 0.019.
Values may be sent and summed in bfloat16 or wider, within the bound.
No kernel may reach another device: no remote copies, remote signals or barrier semaphores. Data moves between devices by JAX's collectives and lax.ppermute only.
A program may use at most 64 MiB of HBM per device.

```python
import math
import jax
import jax.numpy as jnp
import numpy as np
from jax import lax

HEADS = 32
KVH = 8
HDIM = 128
D = 4096
BLOCK = 64
TOKENS = 16384
NBLK = 256
NDOCS = 18
MOSTB = 160


def key_values(key):
    sampled_values = jax.random.normal(jax.random.fold_in(key, 104), (TOKENS, KVH * HDIM), jnp.float32)
    return jnp.clip(sampled_values, -3.5, 3.5)


def draw_key_rows(key, part):
    sampled_values = key_values(key)
    return sampled_values.astype(jnp.bfloat16)


def draw_query_rows(key, part):
    key = jax.random.fold_in(key, 2)
    sampled_values = jnp.clip(jax.random.normal(key, (TOKENS, HEADS * HDIM), jnp.float32), -6.0, 6.0)
    return sampled_values.astype(jnp.bfloat16)


def spiked(drawn, key, source, target, blocks, factor):
    def block_of(dim):
        return (jnp.arange(drawn.shape[dim]) // (drawn.shape[dim] // blocks)).reshape((-1,) + (1,) * (drawn.ndim - 1 - dim))

    first = jax.random.permutation(key, blocks)[block_of(target)]
    other_side = (block_of(target) + blocks // 2) % blocks
    return jnp.where((block_of(source) == first) | (block_of(source) == other_side), factor * drawn, drawn)


def levels(stream_key, extent, split, least, top_value):
    loudness = 1.0
    for dim, parts in split:
        heights = jax.random.uniform(jax.random.fold_in(jax.random.fold_in(stream_key, 6), dim), (parts,), jnp.float32, least / len(split), top_value / len(split))
        loudness = loudness * jnp.repeat(jnp.exp(heights), extent[dim] // parts).reshape((-1,) + (1,) * (len(extent) - 1 - dim))
    return loudness


def split_up(count, total, most, lean):
    portions = [(1 << 20) // math.isqrt(rank ** lean) + 1 for rank in range(2, count + 1)]
    rest, given = total - most - (count - 1), [1] * (count - 1)
    while rest > 0:
        movable = [i for i in range(count - 1) if given[i] < most]
        mass, left = sum([portions[i] for i in movable]), rest
        for i in movable:
            addition = min(most - given[i], max(1, left * portions[i] // mass), rest)
            given[i] = given[i] + addition
            rest = rest - addition
    return np.array([most] + given)


def uneven(stream_key, amount, total, most, slope):
    if amount == 2:
        one = jax.random.randint(stream_key, (), max(1, total - most), min(most, total - 1) + 1)
        return jnp.stack([one, total - one])
    tallies = jnp.asarray(split_up(amount, total, most, slope), jnp.int32)
    pairs = (amount - 1) // 2
    source_of, receiver = tallies[1:1 + 2 * pairs:2], tallies[2:2 + 2 * pairs:2]
    room = jnp.minimum(source_of - 1, most - receiver)
    shifted = jax.random.randint(jax.random.fold_in(stream_key, 1), (pairs,), 0, 1 << 20) % (room + 1)
    tallies = tallies.at[1:1 + 2 * pairs:2].set(source_of - shifted).at[2:2 + 2 * pairs:2].set(receiver + shifted)
    return tallies[jax.random.permutation(jax.random.fold_in(stream_key, 2), amount)]


def normal_values(own_key, extent, deviation, most, split=(), kind=jnp.bfloat16):
    values = deviation * jax.random.normal(own_key, extent, jnp.float32)
    if split:
        values = values * levels(own_key, extent, split, -0.22, 0.18)
    return jnp.clip(values, -most, most).astype(kind)


def noise_with(key, extent, deviation, most, cuts, heavy, held_as=jnp.bfloat16):
    values = deviation * jax.random.normal(key, extent, jnp.float32)
    if cuts:
        values = values * levels(key, extent, cuts, -0.22, 0.18)
    return jnp.clip(spiked(values, jax.random.fold_in(key, 3), *heavy), -most, most).astype(held_as)


def setup_inputs(seed: int = 0) -> dict:
    key_of = jax.random.split(jax.random.key(seed), 6)
    query_rows = draw_query_rows(jax.random.fold_in(key_of[5], 71), 0)
    key_rows = draw_key_rows(jax.random.fold_in(key_of[5], 71), 0)
    value_rows = normal_values(key_of[2], (TOKENS, KVH * HDIM), 1.0, 6.0, ((0, 64), (1, 8)))
    doc_ids = jnp.searchsorted(jnp.cumsum(uneven(key_of[3], NDOCS, NBLK, MOSTB, 2)), jnp.arange(NBLK), side="right").astype(jnp.int32)
    out_weight = noise_with(key_of[4], (HEADS * HDIM, D), (HEADS * HDIM) ** -0.5, 0.125, ((0, 8),), (0, 1, 8, 2.0))
    return dict(query_rows=query_rows, key_rows=key_rows, value_rows=value_rows, doc_ids=doc_ids, out_weight=out_weight)


NEG_BIG = -1.0e30


def attention_reference(query_rows, key_rows, value_rows, doc_ids):
    group_size = HEADS // KVH
    query_block = min(TOKENS, 256)
    block_total = TOKENS // query_block
    score_scale = 1.0 / (HDIM ** 0.5)
    token_docs = jnp.repeat(doc_ids, BLOCK)
    key_pos = jnp.arange(TOKENS, dtype=jnp.int32)
    key_heads = key_rows.astype(jnp.float32).reshape(TOKENS, KVH, HDIM).transpose(1, 0, 2)
    value_heads = value_rows.astype(jnp.float32).reshape(TOKENS, KVH, HDIM).transpose(1, 0, 2)
    query_all = query_rows.astype(jnp.float32).reshape(TOKENS, KVH, group_size, HDIM)

    def one_block(block_index):
        leading_row = (block_index * query_block).astype(jnp.int32)
        query_part = lax.dynamic_slice_in_dim(query_all, leading_row, query_block, 0)
        query_pos = leading_row + jnp.arange(query_block, dtype=jnp.int32)
        query_doc = lax.dynamic_slice_in_dim(token_docs, leading_row, query_block, 0)
        visible = (key_pos[None, :] <= query_pos[:, None]) & (token_docs[None, :] == query_doc[:, None])

        def one_head(head_inputs):
            head_queries, head_keys, head_values = head_inputs
            scores = jnp.einsum("tgd,sd->gts", head_queries, head_keys) * score_scale
            scores = jnp.where(visible[None], scores, NEG_BIG)
            row_max = jnp.max(scores, axis=-1, keepdims=True)
            weights = jnp.where(visible[None], jnp.exp(scores - row_max), 0.0)
            row_sum = jnp.sum(weights, axis=-1)
            rounded = lax.optimization_barrier(weights.astype(jnp.bfloat16)).astype(jnp.float32)
            summed = jnp.einsum("gts,sd->tgd", rounded, head_values)
            return summed / row_sum.T[:, :, None]

        return lax.map(one_head, (query_part.transpose(1, 0, 2, 3), key_heads, value_heads))

    blocks_out = lax.map(one_block, jnp.arange(block_total, dtype=jnp.int32))
    return blocks_out.transpose(0, 2, 1, 3, 4).reshape(TOKENS, HEADS * HDIM).astype(jnp.bfloat16)


def reference(query_rows, key_rows, value_rows, doc_ids, out_weight):
    attended = attention_reference(query_rows, key_rows, value_rows, doc_ids)
    projected = jnp.dot(attended, out_weight, preferred_element_type=jnp.float32).astype(jnp.bfloat16)
    return attended, projected
```

```python
import functools
import math

import jax
import jax.numpy as jnp
from jax import lax
from jax.experimental import pallas as pl
from jax.experimental.pallas import tpu as pltpu
from jax.sharding import PartitionSpec as P

HDIM = 128
BLOCK = 64
ROWS = 256
GROUP = 4
NZ, NX, NC = 8, 4, 2
QCOLS = GROUP * ROWS
PAD = 16
NEG_BIG = -1e30
SCALE = math.log2(math.e) / math.sqrt(HDIM)

X_GROUPS = [[(z * NX + x) * NC + c for x in range(NX)] for z in range(NZ) for c in range(NC)]
Z_GROUPS = [[(z * NX + x) * NC + c for z in range(NZ)] for x in range(NX) for c in range(NC)]


def ctx_perm(move):
    pairs = []
    for index in range(NZ * NX * NC):
        z, x, c = index // (NX * NC), (index // NC) % NX, index % NC
        z, x, c = move(z, x, c)
        pairs.append((index, ((z % NZ) * NX + x % NX) * NC + c % NC))
    return pairs


def attend_kernel(
    place, q_ids, own_ids, other_ids, q0, q1, q2, q3, kv_own, kv_other,
    out, v_turned, total, high, norm,
):
    index = place[0]
    z, x, c = lax.div(index, NX * NC), lax.rem(lax.div(index, NC), NX), lax.rem(index, NC)
    queries = (q0, q1, q2, q3)

    def turn(zk, carry):
        v_turned[zk, :, 0:ROWS] = kv_own[zk, ROWS : 2 * ROWS, :].T
        v_turned[zk, :, ROWS : 2 * ROWS] = kv_other[zk, ROWS : 2 * ROWS, :].T
        return carry

    lax.fori_loop(0, z + 1, turn, 0)

    for r in range(NX):
        q_ref = queries[r]
        xq = lax.rem(x - r + NX, NX)
        q_first = ((z * NX + xq) * NC + c) * ROWS
        total[...] = jnp.zeros_like(total)
        high[...] = jnp.full_like(high, NEG_BIG)
        norm[...] = jnp.zeros_like(norm)

        def fold(zk, masked):
            if masked:
                key_first = (zk * NX + x) * (NC * ROWS)
                q_block = lax.broadcasted_iota(jnp.int32, (1, ROWS), 1)
                low = jnp.zeros((1, ROWS), jnp.int32)
                for b in range(ROWS // BLOCK):
                    before = jnp.int32(0)
                    for kb in range(ROWS // BLOCK):
                        before += jnp.where(own_ids[zk, kb] < q_ids[r, b], 1, 0)
                        before += jnp.where(other_ids[zk, kb] < q_ids[r, b], 1, 0)
                    low = jnp.where(q_block >= b * BLOCK, key_first + before * BLOCK, low)
                q_pos = q_first + q_block
                rows = lax.broadcasted_iota(jnp.int32, (ROWS, ROWS), 0)
                pos_own = rows + (key_first + c * ROWS)
                pos_other = rows + (key_first + (1 - c) * ROWS)
                seen_own = (pos_own >= low) & (pos_own <= q_pos)
                seen_other = (pos_other >= low) & (pos_other <= q_pos)
            k_own = kv_own[zk, 0:ROWS, :]
            k_other = kv_other[zk, 0:ROWS, :]
            for h in range(GROUP):
                cols = slice(h * ROWS, (h + 1) * ROWS)
                q_head = q_ref[0:ROWS, h * HDIM : (h + 1) * HDIM]
                dims = (((1,), (1,)), ((), ()))
                s_own = lax.dot_general(k_own, q_head, dims, preferred_element_type=jnp.float32)
                s_other = lax.dot_general(k_other, q_head, dims, preferred_element_type=jnp.float32)
                if masked:
                    s_own = jnp.where(seen_own, s_own, NEG_BIG)
                    s_other = jnp.where(seen_other, s_other, NEG_BIG)
                old = high[0:1, cols]
                new = jnp.maximum(
                    jnp.max(jnp.maximum(s_own, s_other), axis=0, keepdims=True), old
                )
                factor = jnp.exp2((old - new) * SCALE)
                p_own = jnp.exp2((s_own - new) * SCALE)
                p_other = jnp.exp2((s_other - new) * SCALE)
                if masked:
                    p_own = jnp.where(seen_own, p_own, 0.0)
                    p_other = jnp.where(seen_other, p_other, 0.0)
                high[0:1, cols] = new
                norm[0:1, cols] = norm[0:1, cols] * factor + jnp.sum(
                    p_own + p_other, axis=0, keepdims=True
                )
                update = jnp.dot(
                    v_turned[zk, :, 0:ROWS],
                    p_own.astype(jnp.bfloat16),
                    preferred_element_type=jnp.float32,
                ) + jnp.dot(
                    v_turned[zk, :, ROWS : 2 * ROWS],
                    p_other.astype(jnp.bfloat16),
                    preferred_element_type=jnp.float32,
                )
                total[:, cols] = total[:, cols] * factor + update

        def step(zk, carry):
            key_first = (zk * NX + x) * (NC * ROWS)
            k_low = jnp.minimum(own_ids[zk, 0], other_ids[zk, 0])
            k_top = jnp.maximum(own_ids[zk, 3], other_ids[zk, 3])
            q_low, q_top = q_ids[r, 0], q_ids[r, 3]
            some = (key_first <= q_first + ROWS - 1) & (k_top >= q_low)
            whole = (key_first + NC * ROWS - 1 <= q_first) & (k_low == q_top)

            @pl.when(some & whole)
            def _():
                fold(zk, False)

            @pl.when(some & jnp.logical_not(whole))
            def _():
                fold(zk, True)

            return carry

        lax.fori_loop(0, z + 1, step, 0)

        sums = norm[0:1, :]
        seen = sums > 0.0
        safe = jnp.where(seen, sums, 1.0)
        level = jnp.where(seen, high[0:1, :] * SCALE + jnp.log2(safe), NEG_BIG)
        first = level.astype(jnp.bfloat16).astype(jnp.float32)
        rest = level - first
        second = rest.astype(jnp.bfloat16).astype(jnp.float32)
        third = rest - second
        row = lax.broadcasted_iota(jnp.int32, (PAD, QCOLS), 0)
        stats = jnp.where(row == 0, first, jnp.where(row == 1, second, jnp.where(row == 2, third, 0.0)))
        out[xq, 0:HDIM, :] = (total[...] * (1.0 / safe)).astype(jnp.bfloat16)
        out[xq, HDIM : HDIM + PAD, :] = stats.astype(jnp.bfloat16)


def attend(place, q_ids, own_ids, other_ids, blocks, kv_own, kv_other):
    smem = pl.BlockSpec(memory_space=pltpu.SMEM)
    vmem = pl.BlockSpec(memory_space=pltpu.VMEM)
    return pl.pallas_call(
        attend_kernel,
        out_shape=jax.ShapeDtypeStruct((NX, HDIM + PAD, QCOLS), jnp.bfloat16),
        in_specs=[smem] * 4 + [vmem] * 6,
        out_specs=vmem,
        scratch_shapes=[
            pltpu.VMEM((NZ, HDIM, NC * ROWS), jnp.bfloat16),
            pltpu.VMEM((HDIM, QCOLS), jnp.float32),
            pltpu.VMEM((8, QCOLS), jnp.float32),
            pltpu.VMEM((8, QCOLS), jnp.float32),
        ],
        compiler_params=pltpu.CompilerParams(vmem_limit_bytes=24 * 1024 * 1024),
    )(place, q_ids, own_ids, other_ids, *blocks, kv_own, kv_other)


def project_kernel(parts, weight, attended, partial):
    levels = []
    for s in range(NX):
        stats = parts[s, HDIM : HDIM + PAD, :].astype(jnp.float32)
        levels.append(stats[0:1, :] + stats[1:2, :] + stats[2:3, :])
    top = functools.reduce(jnp.maximum, levels)
    shares = [jnp.exp2(level - top) for level in levels]
    inverse = 1.0 / sum(shares)
    mixed = sum(
        parts[s, 0:HDIM, :].astype(jnp.float32) * (shares[s] * inverse) for s in range(NX)
    )
    for h in range(GROUP):
        block = mixed[:, h * ROWS : (h + 1) * ROWS]
        attended[:, h * HDIM : (h + 1) * HDIM] = block.T.astype(jnp.bfloat16)
    width = 512
    for n in range(partial.shape[1] // width):
        cols = slice(n * width, (n + 1) * width)
        partial[:, cols] = jnp.dot(
            attended[...], weight[:, cols], preferred_element_type=jnp.float32
        ).astype(jnp.bfloat16)


def project(parts, weight):
    vmem = pl.BlockSpec(memory_space=pltpu.VMEM)
    return pl.pallas_call(
        project_kernel,
        out_shape=(
            jax.ShapeDtypeStruct((ROWS, GROUP * HDIM), jnp.bfloat16),
            jax.ShapeDtypeStruct((ROWS, weight.shape[1]), jnp.bfloat16),
        ),
        in_specs=[vmem] * 2,
        out_specs=(vmem, vmem),
        compiler_params=pltpu.CompilerParams(vmem_limit_bytes=24 * 1024 * 1024),
    )(parts, weight)


def per_device(query_rows, key_rows, value_rows, doc_ids, out_weight):
    place = lax.axis_index("ctx").reshape(1)
    ids = doc_ids.astype(jnp.bfloat16)[None, :]

    q_packed = jnp.concatenate(
        [query_rows, jnp.pad(ids, ((0, PAD - 1), (0, query_rows.shape[1] - 4)))], axis=0
    )
    q_blocks = [q_packed] + [
        lax.ppermute(q_packed, "ctx", ctx_perm(lambda z, x, c, r=r: (z, x + r, c)))
        for r in range(1, NX)
    ]
    kv_packed = jnp.concatenate(
        [key_rows, value_rows, jnp.pad(ids, ((0, PAD - 1), (0, HDIM - 4)))], axis=0
    )
    kv_own = lax.all_to_all(
        jnp.broadcast_to(kv_packed[None], (NZ,) + kv_packed.shape),
        "ctx",
        0,
        0,
        axis_index_groups=Z_GROUPS,
    )
    kv_other = lax.ppermute(kv_own, "ctx", ctx_perm(lambda z, x, c: (z, x, 1 - c)))

    q_ids = jnp.stack([block[ROWS, 0:4] for block in q_blocks]).astype(jnp.int32)
    own_ids = kv_own[:, 2 * ROWS, 0:4].astype(jnp.int32)
    other_ids = kv_other[:, 2 * ROWS, 0:4].astype(jnp.int32)
    parts = attend(place, q_ids, own_ids, other_ids, q_blocks, kv_own, kv_other)
    parts = lax.all_to_all(parts, "ctx", 0, 0, axis_index_groups=X_GROUPS)
    attended, partial = project(parts, out_weight)
    projected = lax.psum_scatter(partial, "hd", scatter_dimension=1, tiled=True)
    return attended, projected


def solution(mesh):
    in_specs = (P("ctx", "hd"), P("ctx", "hd"), P("ctx", "hd"), P("ctx"), P("hd", None))
    out_specs = (P("ctx", "hd"), P("ctx", "hd"))
    return jax.shard_map(
        per_device, mesh=mesh, in_specs=in_specs, out_specs=out_specs, check_vma=False
    )
```

```python
import functools
import math

import jax
import jax.numpy as jnp
from jax import lax
from jax.experimental import pallas as pl
from jax.experimental.pallas import tpu as pltpu
from jax.sharding import PartitionSpec as P

HDIM = 128
BLOCK = 64
ROWS = 256
GROUP = 4
NZ, NX, NC = 8, 4, 2
QCOLS = GROUP * ROWS
PAD = 16
NEG_BIG = -1e30
SCALE = math.log2(math.e) / math.sqrt(HDIM)

X_GROUPS = [[(z * NX + x) * NC + c for x in range(NX)] for z in range(NZ) for c in range(NC)]
Z_GROUPS = [[(z * NX + x) * NC + c for z in range(NZ)] for x in range(NX) for c in range(NC)]


def ctx_perm(move):
    pairs = []
    for index in range(NZ * NX * NC):
        z, x, c = index // (NX * NC), (index // NC) % NX, index % NC
        z, x, c = move(z, x, c)
        pairs.append((index, ((z % NZ) * NX + x % NX) * NC + c % NC))
    return pairs


def attend_kernel(
    place, q_ids, own_ids, other_ids, q0, q1, q2, q3, kv_own, kv_other,
    out, q_held, k_held, v_turned, scores, total, high, norm,
):
    index = place[0]
    z, x, c = lax.div(index, NX * NC), lax.rem(lax.div(index, NC), NX), lax.rem(index, NC)
    own_at, other_at = pl.multiple_of(c * ROWS, ROWS), pl.multiple_of((1 - c) * ROWS, ROWS)

    for r, q_ref in enumerate((q0, q1, q2, q3)):
        for h in range(GROUP):
            q_held[r, h * ROWS : (h + 1) * ROWS, :] = q_ref[0:ROWS, h * HDIM : (h + 1) * HDIM]

    def hold(zk, carry):
        k_held[zk, pl.ds(own_at, ROWS), :] = kv_own[zk, 0:ROWS, :]
        k_held[zk, pl.ds(other_at, ROWS), :] = kv_other[zk, 0:ROWS, :]
        v_turned[zk, :, pl.ds(own_at, ROWS)] = kv_own[zk, ROWS : 2 * ROWS, :].T
        v_turned[zk, :, pl.ds(other_at, ROWS)] = kv_other[zk, ROWS : 2 * ROWS, :].T
        return carry

    lax.fori_loop(0, z + 1, hold, 0)

    def multiply(r, zk):
        return lax.dot_general(
            k_held[zk], q_held[r], (((1,), (1,)), ((), ())), preferred_element_type=jnp.float32
        )

    def one_block(r, carry):
        xq = lax.rem(x - r + NX, NX)
        q_first = ((z * NX + xq) * NC + c) * ROWS
        q_low, q_top = q_ids[r, 0], q_ids[r, ROWS // BLOCK - 1]
        total[...] = jnp.zeros_like(total)
        high[...] = jnp.full_like(high, NEG_BIG)
        norm[...] = jnp.zeros_like(norm)

        start = jnp.int32(0)
        for zk in range(NZ):
            k_top = jnp.maximum(own_ids[zk, 3], other_ids[zk, 3])
            start += jnp.where((k_top < q_low) & (zk < z), 1, 0)
        stop = jnp.where(xq < x, z, z + 1)

        def fold(slot, zk, masked):
            if masked:
                key_first = (zk * NX + x) * (NC * ROWS)
                token = lax.rem(lax.broadcasted_iota(jnp.int32, (1, QCOLS), 1), ROWS)
                low = jnp.zeros((1, QCOLS), jnp.int32)
                for b in range(ROWS // BLOCK):
                    before = jnp.int32(0)
                    for kb in range(ROWS // BLOCK):
                        before += jnp.where(own_ids[zk, kb] < q_ids[r, b], 1, 0)
                        before += jnp.where(other_ids[zk, kb] < q_ids[r, b], 1, 0)
                    low = jnp.where(token >= b * BLOCK, before * BLOCK, low)
                last = token + (q_first - key_first)
            scores[1 - slot] = multiply(r, jnp.minimum(zk + 1, z))
            now = scores[slot]
            if masked:
                row = lax.broadcasted_iota(jnp.int32, (NC * ROWS, QCOLS), 0)
                now = jnp.where((row >= low) & (row <= last), now, NEG_BIG)
            old = high[0:1, :]
            new = jnp.maximum(jnp.max(now, axis=0, keepdims=True), old)
            factor = jnp.exp2((old - new) * SCALE)
            weights = jnp.exp2((now - new) * SCALE)
            high[0:1, :] = new
            norm[0:1, :] = norm[0:1, :] * factor + jnp.sum(weights, axis=0, keepdims=True)
            total[...] = total[...] * factor + jnp.dot(
                v_turned[zk], weights.astype(jnp.bfloat16), preferred_element_type=jnp.float32
            )

        def turn(slot, zk):
            at = jnp.minimum(zk, NZ - 1)
            k_low = jnp.minimum(own_ids[at, 0], other_ids[at, 0])
            whole = (k_low == q_top) & ((zk < z) | (xq > x))

            @pl.when((zk < stop) & whole)
            def _():
                fold(slot, zk, False)

            @pl.when((zk < stop) & jnp.logical_not(whole))
            def _():
                fold(slot, zk, True)

        def two_turns(i, inner):
            turn(0, start + 2 * i)
            turn(1, start + 2 * i + 1)
            return inner

        @pl.when(start < stop)
        def _():
            scores[0] = multiply(r, start)

        lax.fori_loop(0, lax.div(jnp.maximum(stop - start, 0) + 1, 2), two_turns, 0)

        seen = high[0:1, :] > NEG_BIG
        safe = jnp.where(seen, norm[0:1, :], 1.0)
        share = jnp.where(seen, 1.0 / safe, 0.0)
        level = jnp.where(seen, high[0:1, :] * SCALE + jnp.log2(safe), NEG_BIG)
        first = level.astype(jnp.bfloat16).astype(jnp.float32)
        rest = level - first
        second = rest.astype(jnp.bfloat16).astype(jnp.float32)
        third = rest - second
        row = lax.broadcasted_iota(jnp.int32, (PAD, QCOLS), 0)
        stats = jnp.where(row == 0, first, jnp.where(row == 1, second, jnp.where(row == 2, third, 0.0)))
        out[xq, 0:HDIM, :] = (total[...] * share).astype(jnp.bfloat16)
        out[xq, HDIM : HDIM + PAD, :] = stats.astype(jnp.bfloat16)
        return carry

    lax.fori_loop(0, NX, one_block, 0)


def attend(place, q_ids, own_ids, other_ids, blocks, kv_own, kv_other):
    smem = pl.BlockSpec(memory_space=pltpu.SMEM)
    vmem = pl.BlockSpec(memory_space=pltpu.VMEM)
    return pl.pallas_call(
        attend_kernel,
        out_shape=jax.ShapeDtypeStruct((NX, HDIM + PAD, QCOLS), jnp.bfloat16),
        in_specs=[smem] * 4 + [vmem] * 6,
        out_specs=vmem,
        scratch_shapes=[
            pltpu.VMEM((NX, QCOLS, HDIM), jnp.bfloat16),
            pltpu.VMEM((NZ, NC * ROWS, HDIM), jnp.bfloat16),
            pltpu.VMEM((NZ, HDIM, NC * ROWS), jnp.bfloat16),
            pltpu.VMEM((2, NC * ROWS, QCOLS), jnp.float32),
            pltpu.VMEM((HDIM, QCOLS), jnp.float32),
            pltpu.VMEM((8, QCOLS), jnp.float32),
            pltpu.VMEM((8, QCOLS), jnp.float32),
        ],
        compiler_params=pltpu.CompilerParams(vmem_limit_bytes=32 * 1024 * 1024),
    )(place, q_ids, own_ids, other_ids, *blocks, kv_own, kv_other)


def project_kernel(parts, weight, attended, partial):
    levels = []
    for s in range(NX):
        stats = parts[s, HDIM : HDIM + PAD, :].astype(jnp.float32)
        levels.append(stats[0:1, :] + stats[1:2, :] + stats[2:3, :])
    top = functools.reduce(jnp.maximum, levels)
    shares = [jnp.exp2(level - top) for level in levels]
    inverse = 1.0 / sum(shares)
    mixed = sum(
        parts[s, 0:HDIM, :].astype(jnp.float32) * (shares[s] * inverse) for s in range(NX)
    )
    for h in range(GROUP):
        block = mixed[:, h * ROWS : (h + 1) * ROWS]
        attended[:, h * HDIM : (h + 1) * HDIM] = block.T.astype(jnp.bfloat16)
    width = 512
    for n in range(partial.shape[1] // width):
        cols = slice(n * width, (n + 1) * width)
        partial[:, cols] = jnp.dot(
            attended[...], weight[:, cols], preferred_element_type=jnp.float32
        ).astype(jnp.bfloat16)


def project(parts, weight):
    vmem = pl.BlockSpec(memory_space=pltpu.VMEM)
    return pl.pallas_call(
        project_kernel,
        out_shape=(
            jax.ShapeDtypeStruct((ROWS, GROUP * HDIM), jnp.bfloat16),
            jax.ShapeDtypeStruct((ROWS, weight.shape[1]), jnp.bfloat16),
        ),
        in_specs=[vmem] * 2,
        out_specs=(vmem, vmem),
        compiler_params=pltpu.CompilerParams(vmem_limit_bytes=24 * 1024 * 1024),
    )(parts, weight)


def per_device(query_rows, key_rows, value_rows, doc_ids, out_weight):
    place = lax.axis_index("ctx").reshape(1)
    ids = doc_ids.astype(jnp.bfloat16)[None, :]

    q_packed = jnp.concatenate(
        [query_rows, jnp.pad(ids, ((0, PAD - 1), (0, query_rows.shape[1] - 4)))], axis=0
    )
    q_blocks = [q_packed] + [
        lax.ppermute(q_packed, "ctx", ctx_perm(lambda z, x, c, r=r: (z, x + r, c)))
        for r in range(1, NX)
    ]
    kv_packed = jnp.concatenate(
        [key_rows, value_rows, jnp.pad(ids, ((0, PAD - 1), (0, HDIM - 4)))], axis=0
    )
    kv_own = lax.all_to_all(
        jnp.broadcast_to(kv_packed[None], (NZ,) + kv_packed.shape),
        "ctx",
        0,
        0,
        axis_index_groups=Z_GROUPS,
    )
    *q_blocks, kv_own = lax.optimization_barrier((*q_blocks, kv_own))
    kv_other = lax.ppermute(kv_own, "ctx", ctx_perm(lambda z, x, c: (z, x, 1 - c)))

    q_ids = jnp.stack([block[ROWS, 0:4] for block in q_blocks]).astype(jnp.int32)
    own_ids = kv_own[:, 2 * ROWS, 0:4].astype(jnp.int32)
    other_ids = kv_other[:, 2 * ROWS, 0:4].astype(jnp.int32)
    parts = attend(place, q_ids, own_ids, other_ids, q_blocks, kv_own, kv_other)
    parts = lax.all_to_all(parts, "ctx", 0, 0, axis_index_groups=X_GROUPS)
    attended, partial = project(parts, out_weight)
    projected = lax.psum_scatter(partial, "hd", scatter_dimension=1, tiled=True)
    return attended, projected


def solution(mesh):
    in_specs = (P("ctx", "hd"), P("ctx", "hd"), P("ctx", "hd"), P("ctx"), P("hd", None))
    out_specs = (P("ctx", "hd"), P("ctx", "hd"))
    return jax.shard_map(
        per_device, mesh=mesh, in_specs=in_specs, out_specs=out_specs, check_vma=False
    )
```

```python
import functools
import math

import jax
import jax.numpy as jnp
from jax import lax
from jax.experimental import pallas as pl
from jax.experimental.pallas import tpu as pltpu
from jax.sharding import PartitionSpec as P

HDIM = 128
BLOCK = 64
ROWS = 256
GROUP = 4
NZ, NX, NC = 8, 4, 2
NY = 8
QCOLS = GROUP * ROWS
PAD = 16
NEG_BIG = -1e30
SCALE = math.log2(math.e) / math.sqrt(HDIM)

X_GROUPS = [[(z * NX + x) * NC + c for x in range(NX)] for z in range(NZ) for c in range(NC)]
Z_GROUPS = [[(z * NX + x) * NC + c for z in range(NZ)] for x in range(NX) for c in range(NC)]


def ctx_perm(move):
    pairs = []
    for index in range(NZ * NX * NC):
        z, x, c = index // (NX * NC), (index // NC) % NX, index % NC
        z, x, c = move(z, x, c)
        pairs.append((index, ((z % NZ) * NX + x % NX) * NC + c % NC))
    return pairs


def hold_kernel(place, kv_own, kv_other, k_held, v_turned):
    index = place[0]
    z, c = lax.div(index, NX * NC), lax.rem(index, NC)
    own_at, other_at = pl.multiple_of(c * ROWS, ROWS), pl.multiple_of((1 - c) * ROWS, ROWS)

    def hold(zk, carry):
        k_held[zk, pl.ds(own_at, ROWS), :] = kv_own[zk, 0:ROWS, :]
        k_held[zk, pl.ds(other_at, ROWS), :] = kv_other[zk, 0:ROWS, :]
        v_turned[zk, :, pl.ds(own_at, ROWS)] = kv_own[zk, ROWS : 2 * ROWS, :].T
        v_turned[zk, :, pl.ds(other_at, ROWS)] = kv_other[zk, ROWS : 2 * ROWS, :].T
        return carry

    lax.fori_loop(0, z + 1, hold, 0)


def attend_kernel(
    shifts, place, q_ids, own_ids, other_ids, *refs
):
    count = len(shifts)
    q_refs, (k_held, v_turned, out, q_held, bounds, scores, total, high, norm) = refs[:count], refs[count:]
    index = place[0]
    z, x, c = lax.div(index, NX * NC), lax.rem(lax.div(index, NC), NX), lax.rem(index, NC)

    for n, q_ref in enumerate(q_refs):
        for h in range(GROUP):
            q_held[n, h * ROWS : (h + 1) * ROWS, :] = q_ref[0:ROWS, h * HDIM : (h + 1) * HDIM]
        start = jnp.int32(0)
        for zk in range(NZ):
            k_top = jnp.maximum(own_ids[zk, 3], other_ids[zk, 3])
            start += jnp.where((k_top < q_ids[shifts[n], 0]) & (zk < z), 1, 0)
        xq = lax.rem(x - shifts[n] + NX, NX)
        bounds[n, 0] = start
        bounds[n, 1] = jnp.maximum(jnp.where(xq < x, z, z + 1), start + 1)
        bounds[n, 2] = xq
        bounds[n, 3] = shifts[n]
    for k in range(4):
        bounds[count, k] = bounds[count - 1, k]

    def multiply(n, zk):
        return lax.dot_general(
            k_held[zk], q_held[n], (((1,), (1,)), ((), ())), preferred_element_type=jnp.float32
        )

    def fold(slot, n, zk, next_n, next_zk, masked):
        r, xq = bounds[n, 3], bounds[n, 2]
        if masked:
            q_first = ((z * NX + xq) * NC + c) * ROWS
            key_first = (zk * NX + x) * (NC * ROWS)
            token = lax.rem(lax.broadcasted_iota(jnp.int32, (1, QCOLS), 1), ROWS)
            low = jnp.zeros((1, QCOLS), jnp.int32)
            for b in range(ROWS // BLOCK):
                before = jnp.int32(0)
                for kb in range(ROWS // BLOCK):
                    before += jnp.where(own_ids[zk, kb] < q_ids[r, b], 1, 0)
                    before += jnp.where(other_ids[zk, kb] < q_ids[r, b], 1, 0)
                low = jnp.where(token >= b * BLOCK, before * BLOCK, low)
            last = token + (q_first - key_first)
        scores[1 - slot] = multiply(next_n, next_zk)
        now = scores[slot]
        if masked:
            row = lax.broadcasted_iota(jnp.int32, (NC * ROWS, QCOLS), 0)
            now = jnp.where((row >= low) & (row <= last), now, NEG_BIG)
        old = high[0:1, :]
        new = jnp.maximum(jnp.max(now, axis=0, keepdims=True), old)
        factor = jnp.exp2((old - new) * SCALE)
        weights = jnp.exp2((now - new) * SCALE)
        high[0:1, :] = new
        norm[0:1, :] = norm[0:1, :] * factor + jnp.sum(weights, axis=0, keepdims=True)
        total[...] = total[...] * factor + jnp.dot(
            v_turned[zk], weights.astype(jnp.bfloat16), preferred_element_type=jnp.float32
        )

    def clear():
        total[...] = jnp.zeros_like(total)
        high[...] = jnp.full_like(high, NEG_BIG)
        norm[...] = jnp.zeros_like(norm)

    def write(n):
        seen = high[0:1, :] > NEG_BIG
        safe = jnp.where(seen, norm[0:1, :], 1.0)
        share = jnp.where(seen, 1.0 / safe, 0.0)
        level = jnp.where(seen, high[0:1, :] * SCALE + jnp.log2(safe), NEG_BIG)
        first = level.astype(jnp.bfloat16).astype(jnp.float32)
        rest = level - first
        second = rest.astype(jnp.bfloat16).astype(jnp.float32)
        third = rest - second
        row = lax.broadcasted_iota(jnp.int32, (PAD, QCOLS), 0)
        stats = jnp.where(row == 0, first, jnp.where(row == 1, second, jnp.where(row == 2, third, 0.0)))
        at = bounds[n, 2]
        out[at, 0:HDIM, :] = (total[...] * share).astype(jnp.bfloat16)
        out[at, HDIM : HDIM + PAD, :] = stats.astype(jnp.bfloat16)

    def turn(slot, n, zk):
        live = n < count
        at = jnp.minimum(n, count - 1)
        ends = zk + 1 >= bounds[at, 1]
        next_n = jnp.where(ends, n + 1, n)
        next_zk = jnp.where(ends, bounds[jnp.minimum(n + 1, count), 0], zk + 1)
        ready_n = jnp.minimum(next_n, count - 1)
        k_low = jnp.minimum(own_ids[zk, 0], other_ids[zk, 0])
        whole = (k_low == q_ids[bounds[at, 3], ROWS // BLOCK - 1]) & ((zk < z) | (bounds[at, 2] > x))

        @pl.when(live & whole)
        def _():
            fold(slot, at, zk, ready_n, next_zk, False)

        @pl.when(live & jnp.logical_not(whole))
        def _():
            fold(slot, at, zk, ready_n, next_zk, True)

        @pl.when(live & ends)
        def _():
            write(at)
            clear()

        return jnp.where(live, next_n, n), jnp.where(live, next_zk, zk)

    def two_turns(i, carry):
        return turn(1, *turn(0, *carry))

    clear()
    scores[0] = multiply(0, bounds[0, 0])
    tiles = jnp.int32(0)
    for n in range(count):
        tiles += bounds[n, 1] - bounds[n, 0]
    lax.fori_loop(0, lax.div(tiles + 1, 2), two_turns, (jnp.int32(0), bounds[0, 0]))


SMEM = pl.BlockSpec(memory_space=pltpu.SMEM)
VMEM = pl.BlockSpec(memory_space=pltpu.VMEM)


def hold(place, kv_own, kv_other):
    return pl.pallas_call(
        hold_kernel,
        out_shape=(
            jax.ShapeDtypeStruct((NZ, NC * ROWS, HDIM), jnp.bfloat16),
            jax.ShapeDtypeStruct((NZ, HDIM, NC * ROWS), jnp.bfloat16),
        ),
        in_specs=[SMEM, VMEM, VMEM],
        out_specs=(VMEM, VMEM),
        compiler_params=pltpu.CompilerParams(vmem_limit_bytes=24 * 1024 * 1024),
    )(place, kv_own, kv_other)


def attend(shifts, place, q_ids, own_ids, other_ids, q_blocks, k_held, v_turned):
    count = len(shifts)
    pairs = count * NZ * NC * ROWS * QCOLS // 2
    return pl.pallas_call(
        functools.partial(attend_kernel, shifts),
        out_shape=jax.ShapeDtypeStruct((NX, HDIM + PAD, QCOLS), jnp.bfloat16),
        in_specs=[SMEM] * 4 + [VMEM] * (count + 2),
        out_specs=VMEM,
        scratch_shapes=[
            pltpu.VMEM((count, QCOLS, HDIM), jnp.bfloat16),
            pltpu.SMEM((count + 1, 4), jnp.int32),
            pltpu.VMEM((2, NC * ROWS, QCOLS), jnp.float32),
            pltpu.VMEM((HDIM, QCOLS), jnp.float32),
            pltpu.VMEM((8, QCOLS), jnp.float32),
            pltpu.VMEM((8, QCOLS), jnp.float32),
        ],
        compiler_params=pltpu.CompilerParams(vmem_limit_bytes=24 * 1024 * 1024),
        cost_estimate=pl.CostEstimate(
            flops=4 * HDIM * pairs, bytes_accessed=4 * NZ * NC * ROWS * HDIM, transcendentals=pairs
        ),
    )(place, q_ids, own_ids, other_ids, *[q_blocks[r] for r in shifts], k_held, v_turned)


def column_share(attended, weight, y, step, columns):
    width = weight.shape[1] // NY
    at = pl.multiple_of(lax.rem(y + step + NY, NY) * width, width)
    picked = weight[:, pl.ds(at, width)][:, columns]
    return jnp.dot(attended[...], picked, preferred_element_type=jnp.float32).astype(jnp.bfloat16)


def far_kernel(y, parts, weight, attended, ahead3, behind3, ahead4, behind4):
    levels = []
    for s in range(NX):
        stats = parts[s, HDIM : HDIM + PAD, :].astype(jnp.float32)
        levels.append(stats[0:1, :] + stats[1:2, :] + stats[2:3, :])
    top = functools.reduce(jnp.maximum, levels)
    shares = [jnp.exp2(level - top) for level in levels]
    inverse = 1.0 / sum(shares)
    mixed = sum(
        parts[s, 0:HDIM, :].astype(jnp.float32) * (shares[s] * inverse) for s in range(NX)
    )
    for h in range(GROUP):
        block = mixed[:, h * ROWS : (h + 1) * ROWS]
        attended[:, h * HDIM : (h + 1) * HDIM] = block.T.astype(jnp.bfloat16)
    half = ahead4.shape[1]
    everything = slice(0, 2 * half)
    ahead3[...] = column_share(attended, weight, y[0], 3, everything)
    behind3[...] = column_share(attended, weight, y[0], -3, everything)
    ahead4[...] = column_share(attended, weight, y[0], 4, slice(0, half))
    behind4[...] = column_share(attended, weight, y[0], 4, slice(half, 2 * half))


def near_kernel(y, attended, weight, ahead1, behind1, ahead2, behind2, here):
    everything = slice(0, here.shape[1])
    for out, step in ((ahead2, 2), (behind2, -2), (ahead1, 1), (behind1, -1), (here, 0)):
        out[...] = column_share(attended, weight, y[0], step, everything)


def project_far(y, parts, weight):
    width = weight.shape[1] // NY
    whole = jax.ShapeDtypeStruct((ROWS, width), jnp.bfloat16)
    half = jax.ShapeDtypeStruct((ROWS, width // 2), jnp.bfloat16)
    return pl.pallas_call(
        far_kernel,
        out_shape=(
            jax.ShapeDtypeStruct((ROWS, GROUP * HDIM), jnp.bfloat16), whole, whole, half, half,
        ),
        in_specs=[SMEM, VMEM, VMEM],
        out_specs=(VMEM,) * 5,
        compiler_params=pltpu.CompilerParams(vmem_limit_bytes=24 * 1024 * 1024),
        cost_estimate=pl.CostEstimate(
            flops=ROWS * weight.size, bytes_accessed=weight.size, transcendentals=0
        ),
    )(y, parts, weight)


def project_near(y, attended, weight):
    whole = jax.ShapeDtypeStruct((ROWS, weight.shape[1] // NY), jnp.bfloat16)
    return pl.pallas_call(
        near_kernel,
        out_shape=(whole,) * 5,
        in_specs=[SMEM, VMEM, VMEM],
        out_specs=(VMEM,) * 5,
        compiler_params=pltpu.CompilerParams(vmem_limit_bytes=24 * 1024 * 1024),
        cost_estimate=pl.CostEstimate(
            flops=ROWS * weight.size, bytes_accessed=weight.size, transcendentals=0
        ),
    )(y, attended, weight)


def sum_over_hd(far, near):
    ahead3, behind3, ahead4, behind4 = far
    ahead1, behind1, ahead2, behind2, here = near

    def move(rows, step):
        return lax.ppermute(rows, "hd", [(i, (i + step) % NY) for i in range(NY)])

    def wide(rows):
        return rows.astype(jnp.float32)

    half = ahead4.shape[1]
    from3, from_far3 = move(ahead3, 1), move(behind3, -1)
    from4, from_far4 = move(ahead4, 2), move(behind4, -2)
    onward = wide(ahead2) + wide(from3) + jnp.pad(wide(from4), ((0, 0), (0, half)))
    backward = wide(behind2) + wide(from_far3) + jnp.pad(wide(from_far4), ((0, 0), (half, 0)))
    from2 = move(onward.astype(jnp.bfloat16), 2)
    from_far2 = move(backward.astype(jnp.bfloat16), -2)
    from1, from_far1 = move(ahead1, 1), move(behind1, -1)
    total = wide(here) + wide(from1) + wide(from_far1) + wide(from2) + wide(from_far2)
    return total.astype(jnp.bfloat16)


def per_device(query_rows, key_rows, value_rows, doc_ids, out_weight):
    place = lax.axis_index("ctx").reshape(1)
    ids = doc_ids.astype(jnp.bfloat16)[None, :]

    q_packed = jnp.concatenate(
        [query_rows, jnp.pad(ids, ((0, PAD - 1), (0, query_rows.shape[1] - 4)))], axis=0
    )
    q_blocks = [q_packed] + [
        lax.ppermute(q_packed, "ctx", ctx_perm(lambda z, x, c, r=r: (z, x + r, c)))
        for r in range(1, NX)
    ]
    kv_packed = jnp.concatenate(
        [key_rows, value_rows, jnp.pad(ids, ((0, PAD - 1), (0, HDIM - 4)))], axis=0
    )
    kv_own = lax.all_to_all(
        jnp.broadcast_to(kv_packed[None], (NZ,) + kv_packed.shape),
        "ctx",
        0,
        0,
        axis_index_groups=Z_GROUPS,
    )
    *q_blocks, kv_own = lax.optimization_barrier((*q_blocks, kv_own))
    kv_other = lax.ppermute(kv_own, "ctx", ctx_perm(lambda z, x, c: (z, x, 1 - c)))

    q_ids = jnp.stack([block[ROWS, 0:4] for block in q_blocks]).astype(jnp.int32)
    own_ids = kv_own[:, 2 * ROWS, 0:4].astype(jnp.int32)
    other_ids = kv_other[:, 2 * ROWS, 0:4].astype(jnp.int32)
    k_held, v_turned = hold(place, kv_own, kv_other)
    made = attend((0, 1, 2, 3), place, q_ids, own_ids, other_ids, q_blocks, k_held, v_turned)
    parts = lax.all_to_all(made, "ctx", 0, 0, axis_index_groups=X_GROUPS)
    y = lax.axis_index("hd").reshape(1)
    attended, *far = project_far(y, parts, out_weight)
    near = project_near(y, attended, out_weight)
    return attended, sum_over_hd(far, near)


def solution(mesh):
    in_specs = (P("ctx", "hd"), P("ctx", "hd"), P("ctx", "hd"), P("ctx"), P("hd", None))
    out_specs = (P("ctx", "hd"), P("ctx", "hd"))
    return jax.shard_map(
        per_device, mesh=mesh, in_specs=in_specs, out_specs=out_specs, check_vma=False
    )
```

```python
import functools
import math

import jax
import jax.numpy as jnp
from jax import lax
from jax.experimental import pallas as pl
from jax.experimental.pallas import tpu as pltpu
from jax.sharding import PartitionSpec as P

HDIM = 128
BLOCK = 64
ROWS = 256
GROUP = 4
NZ, NX, NC = 8, 4, 2
NY = 8
QCOLS = GROUP * ROWS
FOREIGN = (2, 1, 3)
PAD = 16
NEG_BIG = -1e30
SCALE = math.log2(math.e) / math.sqrt(HDIM)

Z_GROUPS = [[(z * NX + x) * NC + c for z in range(NZ)] for x in range(NX) for c in range(NC)]


def ctx_perm(move):
    pairs = []
    for index in range(NZ * NX * NC):
        z, x, c = index // (NX * NC), (index // NC) % NX, index % NC
        z, x, c = move(z, x, c)
        pairs.append((index, ((z % NZ) * NX + x % NX) * NC + c % NC))
    return pairs


def hold_kernel(place, kv_own, kv_other, k_held, v_turned):
    index = place[0]
    z, c = lax.div(index, NX * NC), lax.rem(index, NC)
    own_at, other_at = pl.multiple_of(c * ROWS, ROWS), pl.multiple_of((1 - c) * ROWS, ROWS)

    def hold(zk, carry):
        k_held[zk, pl.ds(own_at, ROWS), :] = kv_own[zk, 0:ROWS, :]
        k_held[zk, pl.ds(other_at, ROWS), :] = kv_other[zk, 0:ROWS, :]
        v_turned[zk, :, pl.ds(own_at, ROWS)] = kv_own[zk, ROWS : 2 * ROWS, :].T
        v_turned[zk, :, pl.ds(other_at, ROWS)] = kv_other[zk, ROWS : 2 * ROWS, :].T
        return carry

    lax.fori_loop(0, z + 1, hold, 0)


def attend_kernel(
    shifts, place, q_ids, own_ids, other_ids, *refs
):
    count = len(shifts)
    q_refs, (k_held, v_turned) = refs[:count], refs[count : count + 2]
    outs, (q_held, bounds, scores, total, high, norm) = refs[count + 2 : 2 * count + 2], refs[2 * count + 2 :]
    index = place[0]
    z, x, c = lax.div(index, NX * NC), lax.rem(lax.div(index, NC), NX), lax.rem(index, NC)

    for n, q_ref in enumerate(q_refs):
        for h in range(GROUP):
            q_held[n, h * ROWS : (h + 1) * ROWS, :] = q_ref[0:ROWS, h * HDIM : (h + 1) * HDIM]
        start = jnp.int32(0)
        for zk in range(NZ):
            k_top = jnp.maximum(own_ids[zk, 3], other_ids[zk, 3])
            start += jnp.where((k_top < q_ids[shifts[n], 0]) & (zk < z), 1, 0)
        xq = lax.rem(x - shifts[n] + NX, NX)
        bounds[n, 0] = start
        bounds[n, 1] = jnp.maximum(jnp.where(xq < x, z, z + 1), start + 1)
        bounds[n, 2] = xq
        bounds[n, 3] = shifts[n]
    for k in range(4):
        bounds[count, k] = bounds[count - 1, k]

    def multiply(n, zk):
        return lax.dot_general(
            k_held[zk], q_held[n], (((1,), (1,)), ((), ())), preferred_element_type=jnp.float32
        )

    def fold(slot, n, zk, next_n, next_zk, masked):
        r, xq = bounds[n, 3], bounds[n, 2]
        if masked:
            q_first = ((z * NX + xq) * NC + c) * ROWS
            key_first = (zk * NX + x) * (NC * ROWS)
            token = lax.rem(lax.broadcasted_iota(jnp.int32, (1, QCOLS), 1), ROWS)
            low = jnp.zeros((1, QCOLS), jnp.int32)
            for b in range(ROWS // BLOCK):
                before = jnp.int32(0)
                for kb in range(ROWS // BLOCK):
                    before += jnp.where(own_ids[zk, kb] < q_ids[r, b], 1, 0)
                    before += jnp.where(other_ids[zk, kb] < q_ids[r, b], 1, 0)
                low = jnp.where(token >= b * BLOCK, before * BLOCK, low)
            last = token + (q_first - key_first)
        scores[1 - slot] = multiply(next_n, next_zk)
        now = scores[slot]
        if masked:
            row = lax.broadcasted_iota(jnp.int32, (NC * ROWS, QCOLS), 0)
            now = jnp.where((row >= low) & (row <= last), now, NEG_BIG)
        old = high[0:1, :]
        new = jnp.maximum(jnp.max(now, axis=0, keepdims=True), old)
        factor = jnp.exp2((old - new) * SCALE)
        weights = jnp.exp2((now - new) * SCALE)
        high[0:1, :] = new
        norm[0:1, :] = norm[0:1, :] * factor + jnp.sum(weights, axis=0, keepdims=True)
        total[...] = total[...] * factor + jnp.dot(
            v_turned[zk], weights.astype(jnp.bfloat16), preferred_element_type=jnp.float32
        )

    def clear():
        total[...] = jnp.zeros_like(total)
        high[...] = jnp.full_like(high, NEG_BIG)
        norm[...] = jnp.zeros_like(norm)

    def write(n):
        seen = high[0:1, :] > NEG_BIG
        safe = jnp.where(seen, norm[0:1, :], 1.0)
        share = jnp.where(seen, 1.0 / safe, 0.0)
        level = jnp.where(seen, high[0:1, :] * SCALE + jnp.log2(safe), NEG_BIG)
        first = level.astype(jnp.bfloat16).astype(jnp.float32)
        rest = level - first
        second = rest.astype(jnp.bfloat16).astype(jnp.float32)
        third = rest - second
        row = lax.broadcasted_iota(jnp.int32, (PAD, QCOLS), 0)
        stats = jnp.where(row == 0, first, jnp.where(row == 1, second, jnp.where(row == 2, third, 0.0)))
        done, stats = (total[...] * share).astype(jnp.bfloat16), stats.astype(jnp.bfloat16)
        for k, out in enumerate(outs):

            @pl.when(n == k)
            def _():
                out[0:HDIM, :] = done
                out[HDIM : HDIM + PAD, :] = stats

    def turn(slot, n, zk):
        live = n < count
        at = jnp.minimum(n, count - 1)
        ends = zk + 1 >= bounds[at, 1]
        next_n = jnp.where(ends, n + 1, n)
        next_zk = jnp.where(ends, bounds[jnp.minimum(n + 1, count), 0], zk + 1)
        ready_n = jnp.minimum(next_n, count - 1)
        k_low = jnp.minimum(own_ids[zk, 0], other_ids[zk, 0])
        whole = (k_low == q_ids[bounds[at, 3], ROWS // BLOCK - 1]) & ((zk < z) | (bounds[at, 2] > x))

        @pl.when(live & whole)
        def _():
            fold(slot, at, zk, ready_n, next_zk, False)

        @pl.when(live & jnp.logical_not(whole))
        def _():
            fold(slot, at, zk, ready_n, next_zk, True)

        @pl.when(live & ends)
        def _():
            write(at)
            clear()

        return jnp.where(live, next_n, n), jnp.where(live, next_zk, zk)

    def two_turns(i, carry):
        return turn(1, *turn(0, *carry))

    clear()
    scores[0] = multiply(0, bounds[0, 0])
    tiles = jnp.int32(0)
    for n in range(count):
        tiles += bounds[n, 1] - bounds[n, 0]
    lax.fori_loop(0, lax.div(tiles + 1, 2), two_turns, (jnp.int32(0), bounds[0, 0]))


SMEM = pl.BlockSpec(memory_space=pltpu.SMEM)
VMEM = pl.BlockSpec(memory_space=pltpu.VMEM)


def hold(place, kv_own, kv_other):
    return pl.pallas_call(
        hold_kernel,
        out_shape=(
            jax.ShapeDtypeStruct((NZ, NC * ROWS, HDIM), jnp.bfloat16),
            jax.ShapeDtypeStruct((NZ, HDIM, NC * ROWS), jnp.bfloat16),
        ),
        in_specs=[SMEM, VMEM, VMEM],
        out_specs=(VMEM, VMEM),
        compiler_params=pltpu.CompilerParams(vmem_limit_bytes=24 * 1024 * 1024),
    )(place, kv_own, kv_other)


def attend(shifts, place, q_ids, own_ids, other_ids, q_blocks, k_held, v_turned):
    count = len(shifts)
    pairs = count * NZ * NC * ROWS * QCOLS // 2
    return pl.pallas_call(
        functools.partial(attend_kernel, shifts),
        out_shape=(jax.ShapeDtypeStruct((HDIM + PAD, QCOLS), jnp.bfloat16),) * count,
        in_specs=[SMEM] * 4 + [VMEM] * (count + 2),
        out_specs=(VMEM,) * count,
        scratch_shapes=[
            pltpu.VMEM((count, QCOLS, HDIM), jnp.bfloat16),
            pltpu.SMEM((count + 1, 4), jnp.int32),
            pltpu.VMEM((2, NC * ROWS, QCOLS), jnp.float32),
            pltpu.VMEM((HDIM, QCOLS), jnp.float32),
            pltpu.VMEM((8, QCOLS), jnp.float32),
            pltpu.VMEM((8, QCOLS), jnp.float32),
        ],
        compiler_params=pltpu.CompilerParams(vmem_limit_bytes=24 * 1024 * 1024),
        cost_estimate=pl.CostEstimate(
            flops=4 * HDIM * pairs, bytes_accessed=4 * NZ * NC * ROWS * HDIM, transcendentals=pairs
        ),
    )(place, q_ids, own_ids, other_ids, *[q_blocks[r] for r in shifts], k_held, v_turned)


def column_share(attended, weight, y, step, columns):
    width = weight.shape[1] // NY
    at = pl.multiple_of(lax.rem(y + step + NY, NY) * width, width)
    picked = weight[:, pl.ds(at, width)][:, columns]
    return jnp.dot(attended[...], picked, preferred_element_type=jnp.float32).astype(jnp.bfloat16)


def far_kernel(p0, p1, p2, p3, weight, attended, kept, ahead3, behind3, ahead4, behind4):
    views = (p0, p1, p2, p3)
    levels = []
    for view in views:
        stats = view[HDIM : HDIM + PAD, :].astype(jnp.float32)
        levels.append(stats[0:1, :] + stats[1:2, :] + stats[2:3, :])
    top = functools.reduce(jnp.maximum, levels)
    shares = [jnp.exp2(level - top) for level in levels]
    inverse = 1.0 / sum(shares)
    mixed = sum(
        views[s][0:HDIM, :].astype(jnp.float32) * (shares[s] * inverse) for s in range(NX)
    )
    for h in range(GROUP):
        block = mixed[:, h * ROWS : (h + 1) * ROWS].T.astype(jnp.bfloat16)
        attended[:, h * HDIM : (h + 1) * HDIM] = block
        kept[:, h * HDIM : (h + 1) * HDIM] = block
    rows = kept[...]
    at = 0
    for out in (ahead3, behind3, ahead4, behind4):
        width = out.shape[1]
        out[...] = jnp.dot(
            rows, weight[:, at : at + width], preferred_element_type=jnp.float32
        ).astype(jnp.bfloat16)
        at += width


def near_kernel(attended, weight, ahead2, behind2, ahead1, behind1, here):
    width = here.shape[1]
    for n, out in enumerate((ahead2, behind2, ahead1, behind1, here)):
        out[...] = jnp.dot(
            attended[...], weight[:, n * width : (n + 1) * width],
            preferred_element_type=jnp.float32,
        ).astype(jnp.bfloat16)


def columns_of(y, weight, steps):
    width = weight.shape[1] // NY
    return jnp.concatenate(
        [
            lax.dynamic_slice_in_dim(weight, lax.rem(y + step + NY, NY) * width, width, 1)
            for step in steps
        ],
        axis=1,
    )


def project_far(parts, weight):
    width = weight.shape[1] // 3
    attended = jax.ShapeDtypeStruct((ROWS, GROUP * HDIM), jnp.bfloat16)
    whole = jax.ShapeDtypeStruct((ROWS, width), jnp.bfloat16)
    half = jax.ShapeDtypeStruct((ROWS, width // 2), jnp.bfloat16)
    return pl.pallas_call(
        far_kernel,
        out_shape=(attended, attended, whole, whole, half, half),
        in_specs=[VMEM] * 5,
        out_specs=(VMEM,) * 6,
        compiler_params=pltpu.CompilerParams(vmem_limit_bytes=24 * 1024 * 1024),
        cost_estimate=pl.CostEstimate(
            flops=2 * ROWS * weight.size, bytes_accessed=2 * weight.size, transcendentals=0
        ),
    )(*parts, weight)


def project_near(attended, weight):
    whole = jax.ShapeDtypeStruct((ROWS, weight.shape[1] // 5), jnp.bfloat16)
    return pl.pallas_call(
        near_kernel,
        out_shape=(whole,) * 5,
        in_specs=[VMEM] * 2,
        out_specs=(VMEM,) * 5,
        compiler_params=pltpu.CompilerParams(vmem_limit_bytes=24 * 1024 * 1024),
        cost_estimate=pl.CostEstimate(
            flops=2 * ROWS * weight.size, bytes_accessed=2 * weight.size, transcendentals=0
        ),
    )(attended, weight)


def sum_over_hd(far, near):
    ahead3, behind3, ahead4, behind4 = far
    ahead2, behind2, ahead1, behind1, here = near

    def move(rows, step):
        return lax.ppermute(rows, "hd", [(i, (i + step) % NY) for i in range(NY)])

    def wide(rows):
        return rows.astype(jnp.float32)

    half = ahead4.shape[1]
    from3, from_far3 = move(ahead3, 1), move(behind3, -1)
    from4, from_far4 = move(ahead4, 2), move(behind4, -2)
    onward = wide(ahead2) + wide(from3) + jnp.pad(wide(from4), ((0, 0), (0, half)))
    backward = wide(behind2) + wide(from_far3) + jnp.pad(wide(from_far4), ((0, 0), (half, 0)))
    from2 = move(onward.astype(jnp.bfloat16), 2)
    from_far2 = move(backward.astype(jnp.bfloat16), -2)
    from1, from_far1 = move(ahead1, 1), move(behind1, -1)
    total = wide(here) + wide(from1) + wide(from_far1) + wide(from2) + wide(from_far2)
    return total.astype(jnp.bfloat16)


def per_device(query_rows, key_rows, value_rows, doc_ids, out_weight):
    place = lax.axis_index("ctx").reshape(1)
    ids = doc_ids.astype(jnp.bfloat16)[None, :]

    q_packed = jnp.concatenate(
        [query_rows, jnp.pad(ids, ((0, PAD - 1), (0, query_rows.shape[1] - 4)))], axis=0
    )
    q_blocks = [q_packed] + [
        lax.ppermute(q_packed, "ctx", ctx_perm(lambda z, x, c, r=r: (z, x + r, c)))
        for r in range(1, NX)
    ]
    kv_packed = jnp.concatenate(
        [key_rows, value_rows, jnp.pad(ids, ((0, PAD - 1), (0, HDIM - 4)))], axis=0
    )
    kv_own = lax.all_to_all(
        jnp.broadcast_to(kv_packed[None], (NZ,) + kv_packed.shape),
        "ctx",
        0,
        0,
        axis_index_groups=Z_GROUPS,
    )
    y = lax.axis_index("hd")
    *q_blocks, kv_own = lax.optimization_barrier((*q_blocks, kv_own))
    kv_other = lax.ppermute(kv_own, "ctx", ctx_perm(lambda z, x, c: (z, x, 1 - c)))

    q_ids = jnp.stack([block[ROWS, 0:4] for block in q_blocks]).astype(jnp.int32)
    own_ids = kv_own[:, 2 * ROWS, 0:4].astype(jnp.int32)
    other_ids = kv_other[:, 2 * ROWS, 0:4].astype(jnp.int32)
    k_held, v_turned = hold(place, kv_own, kv_other)
    arrays = (place, q_ids, own_ids, other_ids, q_blocks, k_held, v_turned)
    made = dict(zip(FOREIGN, attend(FOREIGN, *arrays)))
    made[1], weight = lax.optimization_barrier((made[1], out_weight))
    parts = {
        r: lax.ppermute(made[r], "ctx", ctx_perm(lambda z, x, c, r=r: (z, x - r, c)))
        for r in FOREIGN
    }
    (parts[0],) = attend((0,), *arrays)
    far_weight = columns_of(y, weight, (3, -3, 4))
    near_weight = columns_of(y, weight, (2, -2, 1, -1, 0))
    attended, kept, *far = project_far([parts[r] for r in range(NX)], far_weight)
    near = project_near(kept, near_weight)
    return attended, sum_over_hd(far, near)


def solution(mesh):
    in_specs = (P("ctx", "hd"), P("ctx", "hd"), P("ctx", "hd"), P("ctx"), P("hd", None))
    out_specs = (P("ctx", "hd"), P("ctx", "hd"))
    return jax.shard_map(
        per_device, mesh=mesh, in_specs=in_specs, out_specs=out_specs, check_vma=False
    )
```

```python
import functools
import math

import jax
import jax.numpy as jnp
from jax import lax
from jax.experimental import pallas as pl
from jax.experimental.pallas import tpu as pltpu
from jax.sharding import PartitionSpec as P

HDIM = 128
BLOCK = 64
ROWS = 256
GROUP = 4
NZ, NX, NC = 8, 4, 2
NY = 8
QCOLS = GROUP * ROWS
FOREIGN = (2, 3, 1)
PAD = 16
NEG_BIG = -1e30
SCALE = math.log2(math.e) / math.sqrt(HDIM)

Z_GROUPS = [[(z * NX + x) * NC + c for z in range(NZ)] for x in range(NX) for c in range(NC)]


def ctx_perm(move):
    pairs = []
    for index in range(NZ * NX * NC):
        z, x, c = index // (NX * NC), (index // NC) % NX, index % NC
        z, x, c = move(z, x, c)
        pairs.append((index, ((z % NZ) * NX + x % NX) * NC + c % NC))
    return pairs


def hold_kernel(place, kv_own, kv_other, k_held, v_turned):
    index = place[0]
    z, c = lax.div(index, NX * NC), lax.rem(index, NC)
    own_at, other_at = pl.multiple_of(c * ROWS, ROWS), pl.multiple_of((1 - c) * ROWS, ROWS)

    def hold(zk, carry):
        k_held[zk, pl.ds(own_at, ROWS), :] = kv_own[zk, 0:ROWS, :]
        k_held[zk, pl.ds(other_at, ROWS), :] = kv_other[zk, 0:ROWS, :]
        v_turned[zk, :, pl.ds(own_at, ROWS)] = kv_own[zk, ROWS : 2 * ROWS, :].T
        v_turned[zk, :, pl.ds(other_at, ROWS)] = kv_other[zk, ROWS : 2 * ROWS, :].T
        return carry

    lax.fori_loop(0, z + 1, hold, 0)


def attend_kernel(
    shifts, place, q_ids, own_ids, other_ids, *refs
):
    count = len(shifts)
    q_refs, (k_held, v_turned) = refs[:count], refs[count : count + 2]
    outs, (q_held, bounds, scores, total, high, norm) = refs[count + 2 : 2 * count + 2], refs[2 * count + 2 :]
    index = place[0]
    z, x, c = lax.div(index, NX * NC), lax.rem(lax.div(index, NC), NX), lax.rem(index, NC)

    for n, q_ref in enumerate(q_refs):
        for h in range(GROUP):
            q_held[n, h * ROWS : (h + 1) * ROWS, :] = q_ref[0:ROWS, h * HDIM : (h + 1) * HDIM]
        start = jnp.int32(0)
        for zk in range(NZ):
            k_top = jnp.maximum(own_ids[zk, 3], other_ids[zk, 3])
            start += jnp.where((k_top < q_ids[shifts[n], 0]) & (zk < z), 1, 0)
        xq = lax.rem(x - shifts[n] + NX, NX)
        bounds[n, 0] = start
        bounds[n, 1] = jnp.maximum(jnp.where(xq < x, z, z + 1), start + 1)
        bounds[n, 2] = xq
        bounds[n, 3] = shifts[n]
    for k in range(4):
        bounds[count, k] = bounds[count - 1, k]

    def multiply(n, zk):
        return lax.dot_general(
            k_held[zk], q_held[n], (((1,), (1,)), ((), ())), preferred_element_type=jnp.float32
        )

    def fold(slot, n, zk, next_n, next_zk, masked):
        r, xq = bounds[n, 3], bounds[n, 2]
        if masked:
            q_first = ((z * NX + xq) * NC + c) * ROWS
            key_first = (zk * NX + x) * (NC * ROWS)
            token = lax.rem(lax.broadcasted_iota(jnp.int32, (1, QCOLS), 1), ROWS)
            low = jnp.zeros((1, QCOLS), jnp.int32)
            for b in range(ROWS // BLOCK):
                before = jnp.int32(0)
                for kb in range(ROWS // BLOCK):
                    before += jnp.where(own_ids[zk, kb] < q_ids[r, b], 1, 0)
                    before += jnp.where(other_ids[zk, kb] < q_ids[r, b], 1, 0)
                low = jnp.where(token >= b * BLOCK, before * BLOCK, low)
            last = token + (q_first - key_first)
        scores[1 - slot] = multiply(next_n, next_zk)
        now = scores[slot]
        if masked:
            row = lax.broadcasted_iota(jnp.int32, (NC * ROWS, QCOLS), 0)
            now = jnp.where((row >= low) & (row <= last), now, NEG_BIG)
        old = high[0:1, :]
        new = jnp.maximum(jnp.max(now, axis=0, keepdims=True), old)
        factor = jnp.exp2((old - new) * SCALE)
        weights = jnp.exp2((now - new) * SCALE)
        high[0:1, :] = new
        norm[0:1, :] = norm[0:1, :] * factor + jnp.sum(weights, axis=0, keepdims=True)
        total[...] = total[...] * factor + jnp.dot(
            v_turned[zk], weights.astype(jnp.bfloat16), preferred_element_type=jnp.float32
        )

    def clear():
        total[...] = jnp.zeros_like(total)
        high[...] = jnp.full_like(high, NEG_BIG)
        norm[...] = jnp.zeros_like(norm)

    def write(n):
        seen = high[0:1, :] > NEG_BIG
        safe = jnp.where(seen, norm[0:1, :], 1.0)
        share = jnp.where(seen, 1.0 / safe, 0.0)
        level = jnp.where(seen, high[0:1, :] * SCALE + jnp.log2(safe), NEG_BIG)
        first = level.astype(jnp.bfloat16).astype(jnp.float32)
        rest = level - first
        second = rest.astype(jnp.bfloat16).astype(jnp.float32)
        third = rest - second
        row = lax.broadcasted_iota(jnp.int32, (PAD, QCOLS), 0)
        stats = jnp.where(row == 0, first, jnp.where(row == 1, second, jnp.where(row == 2, third, 0.0)))
        done, stats = (total[...] * share).astype(jnp.bfloat16), stats.astype(jnp.bfloat16)
        for k, out in enumerate(outs):

            @pl.when(n == k)
            def _():
                out[0:HDIM, :] = done
                out[HDIM : HDIM + PAD, :] = stats

    def turn(slot, n, zk):
        live = n < count
        at = jnp.minimum(n, count - 1)
        ends = zk + 1 >= bounds[at, 1]
        next_n = jnp.where(ends, n + 1, n)
        next_zk = jnp.where(ends, bounds[jnp.minimum(n + 1, count), 0], zk + 1)
        ready_n = jnp.minimum(next_n, count - 1)
        k_low = jnp.minimum(own_ids[zk, 0], other_ids[zk, 0])
        whole = (k_low == q_ids[bounds[at, 3], ROWS // BLOCK - 1]) & ((zk < z) | (bounds[at, 2] > x))

        @pl.when(live & whole)
        def _():
            fold(slot, at, zk, ready_n, next_zk, False)

        @pl.when(live & jnp.logical_not(whole))
        def _():
            fold(slot, at, zk, ready_n, next_zk, True)

        @pl.when(live & ends)
        def _():
            write(at)
            clear()

        return jnp.where(live, next_n, n), jnp.where(live, next_zk, zk)

    def two_turns(i, carry):
        return turn(1, *turn(0, *carry))

    clear()
    scores[0] = multiply(0, bounds[0, 0])
    tiles = jnp.int32(0)
    for n in range(count):
        tiles += bounds[n, 1] - bounds[n, 0]
    lax.fori_loop(0, lax.div(tiles + 1, 2), two_turns, (jnp.int32(0), bounds[0, 0]))


SMEM = pl.BlockSpec(memory_space=pltpu.SMEM)
VMEM = pl.BlockSpec(memory_space=pltpu.VMEM)


def hold(place, kv_own, kv_other):
    return pl.pallas_call(
        hold_kernel,
        out_shape=(
            jax.ShapeDtypeStruct((NZ, NC * ROWS, HDIM), jnp.bfloat16),
            jax.ShapeDtypeStruct((NZ, HDIM, NC * ROWS), jnp.bfloat16),
        ),
        in_specs=[SMEM, VMEM, VMEM],
        out_specs=(VMEM, VMEM),
        compiler_params=pltpu.CompilerParams(vmem_limit_bytes=24 * 1024 * 1024),
    )(place, kv_own, kv_other)


def attend(shifts, place, q_ids, own_ids, other_ids, q_blocks, k_held, v_turned):
    count = len(shifts)
    pairs = count * NZ * NC * ROWS * QCOLS // 2
    return pl.pallas_call(
        functools.partial(attend_kernel, shifts),
        out_shape=(jax.ShapeDtypeStruct((HDIM + PAD, QCOLS), jnp.bfloat16),) * count,
        in_specs=[SMEM] * 4 + [VMEM] * (count + 2),
        out_specs=(VMEM,) * count,
        scratch_shapes=[
            pltpu.VMEM((count, QCOLS, HDIM), jnp.bfloat16),
            pltpu.SMEM((count + 1, 4), jnp.int32),
            pltpu.VMEM((2, NC * ROWS, QCOLS), jnp.float32),
            pltpu.VMEM((HDIM, QCOLS), jnp.float32),
            pltpu.VMEM((8, QCOLS), jnp.float32),
            pltpu.VMEM((8, QCOLS), jnp.float32),
        ],
        compiler_params=pltpu.CompilerParams(vmem_limit_bytes=24 * 1024 * 1024),
        cost_estimate=pl.CostEstimate(
            flops=4 * HDIM * pairs, bytes_accessed=4 * NZ * NC * ROWS * HDIM, transcendentals=pairs
        ),
    )(place, q_ids, own_ids, other_ids, *[q_blocks[r] for r in shifts], k_held, v_turned)


def column_share(attended, weight, y, step, columns):
    width = weight.shape[1] // NY
    at = pl.multiple_of(lax.rem(y + step + NY, NY) * width, width)
    picked = weight[:, pl.ds(at, width)][:, columns]
    return jnp.dot(attended[...], picked, preferred_element_type=jnp.float32).astype(jnp.bfloat16)


def far_kernel(p0, p1, p2, p3, weight, attended, kept, ahead3, behind3, ahead4, behind4):
    views = (p0, p1, p2, p3)
    levels = []
    for view in views:
        stats = view[HDIM : HDIM + PAD, :].astype(jnp.float32)
        levels.append(stats[0:1, :] + stats[1:2, :] + stats[2:3, :])
    top = functools.reduce(jnp.maximum, levels)
    shares = [jnp.exp2(level - top) for level in levels]
    inverse = 1.0 / sum(shares)
    mixed = sum(
        views[s][0:HDIM, :].astype(jnp.float32) * (shares[s] * inverse) for s in range(NX)
    )
    for h in range(GROUP):
        block = mixed[:, h * ROWS : (h + 1) * ROWS].T.astype(jnp.bfloat16)
        attended[:, h * HDIM : (h + 1) * HDIM] = block
        kept[:, h * HDIM : (h + 1) * HDIM] = block
    rows = kept[...]
    at = 0
    for out in (ahead3, behind3, ahead4, behind4):
        width = out.shape[1]
        out[...] = jnp.dot(
            rows, weight[:, at : at + width], preferred_element_type=jnp.float32
        ).astype(jnp.bfloat16)
        at += width


def near_kernel(attended, weight, ahead2, behind2, ahead1, behind1, here):
    width = here.shape[1]
    for n, out in enumerate((ahead2, behind2, ahead1, behind1, here)):
        out[...] = jnp.dot(
            attended[...], weight[:, n * width : (n + 1) * width],
            preferred_element_type=jnp.float32,
        ).astype(jnp.bfloat16)


def columns_of(y, weight, steps):
    width = weight.shape[1] // NY
    return jnp.concatenate(
        [
            lax.dynamic_slice_in_dim(weight, lax.rem(y + step + NY, NY) * width, width, 1)
            for step in steps
        ],
        axis=1,
    )


def project_far(parts, weight):
    width = weight.shape[1] // 3
    attended = jax.ShapeDtypeStruct((ROWS, GROUP * HDIM), jnp.bfloat16)
    whole = jax.ShapeDtypeStruct((ROWS, width), jnp.bfloat16)
    half = jax.ShapeDtypeStruct((ROWS, width // 2), jnp.bfloat16)
    return pl.pallas_call(
        far_kernel,
        out_shape=(attended, attended, whole, whole, half, half),
        in_specs=[VMEM] * 5,
        out_specs=(VMEM,) * 6,
        compiler_params=pltpu.CompilerParams(vmem_limit_bytes=24 * 1024 * 1024),
        cost_estimate=pl.CostEstimate(
            flops=2 * ROWS * weight.size, bytes_accessed=2 * weight.size, transcendentals=0
        ),
    )(*parts, weight)


def project_near(attended, weight):
    whole = jax.ShapeDtypeStruct((ROWS, weight.shape[1] // 5), jnp.bfloat16)
    return pl.pallas_call(
        near_kernel,
        out_shape=(whole,) * 5,
        in_specs=[VMEM] * 2,
        out_specs=(VMEM,) * 5,
        compiler_params=pltpu.CompilerParams(vmem_limit_bytes=24 * 1024 * 1024),
        cost_estimate=pl.CostEstimate(
            flops=2 * ROWS * weight.size, bytes_accessed=2 * weight.size, transcendentals=0
        ),
    )(attended, weight)


def sum_over_hd(far, near):
    ahead3, behind3, ahead4, behind4 = far
    ahead2, behind2, ahead1, behind1, here = near

    def move(rows, step):
        return lax.ppermute(rows, "hd", [(i, (i + step) % NY) for i in range(NY)])

    def wide(rows):
        return rows.astype(jnp.float32)

    half = ahead4.shape[1]
    from3, from_far3 = move(ahead3, 1), move(behind3, -1)
    from4, from_far4 = move(ahead4, 2), move(behind4, -2)
    onward = wide(ahead2) + wide(from3) + jnp.pad(wide(from4), ((0, 0), (0, half)))
    backward = wide(behind2) + wide(from_far3) + jnp.pad(wide(from_far4), ((0, 0), (half, 0)))
    from2 = move(onward.astype(jnp.bfloat16), 2)
    from_far2 = move(backward.astype(jnp.bfloat16), -2)
    from1, from_far1 = move(ahead1, 1), move(behind1, -1)
    total = wide(here) + wide(from1) + wide(from_far1) + wide(from2) + wide(from_far2)
    return total.astype(jnp.bfloat16)


def per_device(query_rows, key_rows, value_rows, doc_ids, out_weight):
    place = lax.axis_index("ctx").reshape(1)

    def id_rows(columns):
        return jnp.pad(doc_ids[None, :], ((0, PAD - 1), (0, columns - 4))).astype(jnp.bfloat16)

    q_packed = jnp.concatenate([query_rows, id_rows(query_rows.shape[1])], axis=0)
    q_blocks = [q_packed] + [
        lax.ppermute(q_packed, "ctx", ctx_perm(lambda z, x, c, r=r: (z, x + r, c)))
        for r in range(1, NX)
    ]
    kv_packed = jnp.concatenate([key_rows, value_rows, id_rows(HDIM)], axis=0)
    kv_own = lax.all_to_all(
        jnp.broadcast_to(kv_packed[None], (NZ,) + kv_packed.shape),
        "ctx",
        0,
        0,
        axis_index_groups=Z_GROUPS,
    )
    y = lax.axis_index("hd")
    *q_blocks, kv_own = lax.optimization_barrier((*q_blocks, kv_own))
    kv_other = lax.ppermute(kv_own, "ctx", ctx_perm(lambda z, x, c: (z, x, 1 - c)))

    q_ids = jnp.stack([block[ROWS, 0:4] for block in q_blocks]).astype(jnp.int32)
    own_ids = kv_own[:, 2 * ROWS, 0:4].astype(jnp.int32)
    other_ids = kv_other[:, 2 * ROWS, 0:4].astype(jnp.int32)
    k_held, v_turned = hold(place, kv_own, kv_other)
    arrays = (place, q_ids, own_ids, other_ids, q_blocks, k_held, v_turned)
    made = dict(zip(FOREIGN, attend(FOREIGN, *arrays)))
    made[2], weight = lax.optimization_barrier((made[2], out_weight))
    parts = {
        r: lax.ppermute(made[r], "ctx", ctx_perm(lambda z, x, c, r=r: (z, x - r, c)))
        for r in FOREIGN
    }
    (parts[0],) = attend((0,), *arrays)
    far_weight = columns_of(y, weight, (3, -3, 4))
    near_weight = columns_of(y, weight, (2, -2, 1, -1, 0))
    attended, kept, *far = project_far([parts[r] for r in (0, 2, 3, 1)], far_weight)
    near = project_near(kept, near_weight)
    return attended, sum_over_hd(far, near)


def solution(mesh):
    in_specs = (P("ctx", "hd"), P("ctx", "hd"), P("ctx", "hd"), P("ctx"), P("hd", None))
    out_specs = (P("ctx", "hd"), P("ctx", "hd"))
    return jax.shard_map(
        per_device, mesh=mesh, in_specs=in_specs, out_specs=out_specs, check_vma=False
    )
```

```python
import functools
import math

import jax
import jax.numpy as jnp
from jax import lax
from jax.experimental import pallas as pl
from jax.experimental.pallas import tpu as pltpu
from jax.sharding import PartitionSpec as P

HDIM = 128
BLOCK = 64
ROWS = 256
GROUP = 4
NZ, NX, NC = 8, 4, 2
NY = 8
QCOLS = GROUP * ROWS
FOREIGN = (2, 1, 3)
PAD = 16
NEG_BIG = -1e30
SCALE = math.log2(math.e) / math.sqrt(HDIM)

Z_GROUPS = [[(z * NX + x) * NC + c for z in range(NZ)] for x in range(NX) for c in range(NC)]


def ctx_perm(move):
    pairs = []
    for index in range(NZ * NX * NC):
        z, x, c = index // (NX * NC), (index // NC) % NX, index % NC
        z, x, c = move(z, x, c)
        pairs.append((index, ((z % NZ) * NX + x % NX) * NC + c % NC))
    return pairs


def hold_kernel(place, kv_own, kv_other, k_held, v_turned):
    index = place[0]
    z, c = lax.div(index, NX * NC), lax.rem(index, NC)
    own_at, other_at = pl.multiple_of(c * ROWS, ROWS), pl.multiple_of((1 - c) * ROWS, ROWS)

    def hold(zk, carry):
        k_held[zk, pl.ds(own_at, ROWS), :] = kv_own[zk, 0:ROWS, :]
        k_held[zk, pl.ds(other_at, ROWS), :] = kv_other[zk, 0:ROWS, :]
        v_turned[zk, :, pl.ds(own_at, ROWS)] = kv_own[zk, ROWS : 2 * ROWS, :].T
        v_turned[zk, :, pl.ds(other_at, ROWS)] = kv_other[zk, ROWS : 2 * ROWS, :].T
        return carry

    lax.fori_loop(0, z + 1, hold, 0)


def attend_kernel(
    shifts, place, q_ids, own_ids, other_ids, *refs
):
    count = len(shifts)
    q_refs, (k_held, v_turned) = refs[:count], refs[count : count + 2]
    outs, (q_held, bounds, scores, total, high, norm) = refs[count + 2 : 2 * count + 2], refs[2 * count + 2 :]
    index = place[0]
    z, x, c = lax.div(index, NX * NC), lax.rem(lax.div(index, NC), NX), lax.rem(index, NC)

    for n, q_ref in enumerate(q_refs):
        for h in range(GROUP):
            q_held[n, h * ROWS : (h + 1) * ROWS, :] = q_ref[0:ROWS, h * HDIM : (h + 1) * HDIM]
        start = jnp.int32(0)
        for zk in range(NZ):
            k_top = jnp.maximum(own_ids[zk, 3], other_ids[zk, 3])
            start += jnp.where((k_top < q_ids[shifts[n], 0]) & (zk < z), 1, 0)
        xq = lax.rem(x - shifts[n] + NX, NX)
        bounds[n, 0] = start
        bounds[n, 1] = jnp.maximum(jnp.where(xq < x, z, z + 1), start + 1)
        bounds[n, 2] = xq
        bounds[n, 3] = shifts[n]
    for k in range(4):
        bounds[count, k] = bounds[count - 1, k]

    def multiply(n, zk):
        return lax.dot_general(
            k_held[zk], q_held[n], (((1,), (1,)), ((), ())), preferred_element_type=jnp.float32
        )

    def fold(slot, n, zk, next_n, next_zk, masked):
        r, xq = bounds[n, 3], bounds[n, 2]
        if masked:
            q_first = ((z * NX + xq) * NC + c) * ROWS
            key_first = (zk * NX + x) * (NC * ROWS)
            token = lax.rem(lax.broadcasted_iota(jnp.int32, (1, QCOLS), 1), ROWS)
            low = jnp.zeros((1, QCOLS), jnp.int32)
            for b in range(ROWS // BLOCK):
                before = jnp.int32(0)
                for kb in range(ROWS // BLOCK):
                    before += jnp.where(own_ids[zk, kb] < q_ids[r, b], 1, 0)
                    before += jnp.where(other_ids[zk, kb] < q_ids[r, b], 1, 0)
                low = jnp.where(token >= b * BLOCK, before * BLOCK, low)
            last = token + (q_first - key_first)
        scores[1 - slot] = multiply(next_n, next_zk)
        now = scores[slot]
        if masked:
            row = lax.broadcasted_iota(jnp.int32, (NC * ROWS, QCOLS), 0)
            now = jnp.where((row >= low) & (row <= last), now, NEG_BIG)
        old = high[0:1, :]
        new = jnp.maximum(jnp.max(now, axis=0, keepdims=True), old)
        factor = jnp.exp2((old - new) * SCALE)
        weights = jnp.exp2((now - new) * SCALE)
        high[0:1, :] = new
        norm[0:1, :] = norm[0:1, :] * factor + jnp.sum(weights, axis=0, keepdims=True)
        total[...] = total[...] * factor + jnp.dot(
            v_turned[zk], weights.astype(jnp.bfloat16), preferred_element_type=jnp.float32
        )

    def clear():
        total[...] = jnp.zeros_like(total)
        high[...] = jnp.full_like(high, NEG_BIG)
        norm[...] = jnp.zeros_like(norm)

    def write(n):
        seen = high[0:1, :] > NEG_BIG
        safe = jnp.where(seen, norm[0:1, :], 1.0)
        share = jnp.where(seen, 1.0 / safe, 0.0)
        level = jnp.where(seen, high[0:1, :] * SCALE + jnp.log2(safe), NEG_BIG)
        first = level.astype(jnp.bfloat16).astype(jnp.float32)
        rest = level - first
        second = rest.astype(jnp.bfloat16).astype(jnp.float32)
        third = rest - second
        row = lax.broadcasted_iota(jnp.int32, (PAD, QCOLS), 0)
        stats = jnp.where(row == 0, first, jnp.where(row == 1, second, jnp.where(row == 2, third, 0.0)))
        done, stats = (total[...] * share).astype(jnp.bfloat16), stats.astype(jnp.bfloat16)
        for k, out in enumerate(outs):

            @pl.when(n == k)
            def _():
                out[0:HDIM, :] = done
                out[HDIM : HDIM + PAD, :] = stats

    def turn(slot, n, zk):
        live = n < count
        at = jnp.minimum(n, count - 1)
        ends = zk + 1 >= bounds[at, 1]
        next_n = jnp.where(ends, n + 1, n)
        next_zk = jnp.where(ends, bounds[jnp.minimum(n + 1, count), 0], zk + 1)
        ready_n = jnp.minimum(next_n, count - 1)
        k_low = jnp.minimum(own_ids[zk, 0], other_ids[zk, 0])
        whole = (k_low == q_ids[bounds[at, 3], ROWS // BLOCK - 1]) & ((zk < z) | (bounds[at, 2] > x))

        @pl.when(live & whole)
        def _():
            fold(slot, at, zk, ready_n, next_zk, False)

        @pl.when(live & jnp.logical_not(whole))
        def _():
            fold(slot, at, zk, ready_n, next_zk, True)

        @pl.when(live & ends)
        def _():
            write(at)
            clear()

        return jnp.where(live, next_n, n), jnp.where(live, next_zk, zk)

    def two_turns(i, carry):
        return turn(1, *turn(0, *carry))

    clear()
    scores[0] = multiply(0, bounds[0, 0])
    tiles = jnp.int32(0)
    for n in range(count):
        tiles += bounds[n, 1] - bounds[n, 0]
    lax.fori_loop(0, lax.div(tiles + 1, 2), two_turns, (jnp.int32(0), bounds[0, 0]))


SMEM = pl.BlockSpec(memory_space=pltpu.SMEM)
VMEM = pl.BlockSpec(memory_space=pltpu.VMEM)


def hold(place, kv_own, kv_other):
    return pl.pallas_call(
        hold_kernel,
        out_shape=(
            jax.ShapeDtypeStruct((NZ, NC * ROWS, HDIM), jnp.bfloat16),
            jax.ShapeDtypeStruct((NZ, HDIM, NC * ROWS), jnp.bfloat16),
        ),
        in_specs=[SMEM, VMEM, VMEM],
        out_specs=(VMEM, VMEM),
        compiler_params=pltpu.CompilerParams(vmem_limit_bytes=24 * 1024 * 1024),
    )(place, kv_own, kv_other)


def attend(shifts, place, q_ids, own_ids, other_ids, q_blocks, k_held, v_turned):
    count = len(shifts)
    pairs = count * NZ * NC * ROWS * QCOLS // 2
    return pl.pallas_call(
        functools.partial(attend_kernel, shifts),
        out_shape=(jax.ShapeDtypeStruct((HDIM + PAD, QCOLS), jnp.bfloat16),) * count,
        in_specs=[SMEM] * 4 + [VMEM] * (count + 2),
        out_specs=(VMEM,) * count,
        scratch_shapes=[
            pltpu.VMEM((count, QCOLS, HDIM), jnp.bfloat16),
            pltpu.SMEM((count + 1, 4), jnp.int32),
            pltpu.VMEM((2, NC * ROWS, QCOLS), jnp.float32),
            pltpu.VMEM((HDIM, QCOLS), jnp.float32),
            pltpu.VMEM((8, QCOLS), jnp.float32),
            pltpu.VMEM((8, QCOLS), jnp.float32),
        ],
        compiler_params=pltpu.CompilerParams(vmem_limit_bytes=24 * 1024 * 1024),
        cost_estimate=pl.CostEstimate(
            flops=4 * HDIM * pairs, bytes_accessed=4 * NZ * NC * ROWS * HDIM, transcendentals=pairs
        ),
    )(place, q_ids, own_ids, other_ids, *[q_blocks[r] for r in shifts], k_held, v_turned)


def column_share(attended, weight, y, step, columns):
    width = weight.shape[1] // NY
    at = pl.multiple_of(lax.rem(y + step + NY, NY) * width, width)
    picked = weight[:, pl.ds(at, width)][:, columns]
    return jnp.dot(attended[...], picked, preferred_element_type=jnp.float32).astype(jnp.bfloat16)


def far_kernel(p0, p1, p2, p3, weight, attended, kept, ahead3, behind3, ahead4, behind4):
    views = (p0, p1, p2, p3)
    levels = []
    for view in views:
        stats = view[HDIM : HDIM + PAD, :].astype(jnp.float32)
        levels.append(stats[0:1, :] + stats[1:2, :] + stats[2:3, :])
    top = functools.reduce(jnp.maximum, levels)
    shares = [jnp.exp2(level - top) for level in levels]
    inverse = 1.0 / sum(shares)
    mixed = sum(
        views[s][0:HDIM, :].astype(jnp.float32) * (shares[s] * inverse) for s in range(NX)
    )
    for h in range(GROUP):
        block = mixed[:, h * ROWS : (h + 1) * ROWS].T.astype(jnp.bfloat16)
        attended[:, h * HDIM : (h + 1) * HDIM] = block
        kept[:, h * HDIM : (h + 1) * HDIM] = block
    rows = kept[...]
    at = 0
    for out in (ahead3, behind3, ahead4, behind4):
        width = out.shape[1]
        out[...] = jnp.dot(
            rows, weight[:, at : at + width], preferred_element_type=jnp.float32
        ).astype(jnp.bfloat16)
        at += width


def near_kernel(attended, weight, ahead2, behind2, ahead1, behind1, here):
    width = here.shape[1]
    for n, out in enumerate((ahead2, behind2, ahead1, behind1, here)):
        out[...] = jnp.dot(
            attended[...], weight[:, n * width : (n + 1) * width],
            preferred_element_type=jnp.float32,
        ).astype(jnp.bfloat16)


def columns_of(y, weight, steps):
    width = weight.shape[1] // NY
    return jnp.concatenate(
        [
            lax.dynamic_slice_in_dim(weight, lax.rem(y + step + NY, NY) * width, width, 1)
            for step in steps
        ],
        axis=1,
    )


def project_far(parts, weight):
    width = weight.shape[1] // 3
    attended = jax.ShapeDtypeStruct((ROWS, GROUP * HDIM), jnp.bfloat16)
    whole = jax.ShapeDtypeStruct((ROWS, width), jnp.bfloat16)
    half = jax.ShapeDtypeStruct((ROWS, width // 2), jnp.bfloat16)
    return pl.pallas_call(
        far_kernel,
        out_shape=(attended, attended, whole, whole, half, half),
        in_specs=[VMEM] * 5,
        out_specs=(VMEM,) * 6,
        compiler_params=pltpu.CompilerParams(vmem_limit_bytes=24 * 1024 * 1024),
        cost_estimate=pl.CostEstimate(
            flops=2 * ROWS * weight.size, bytes_accessed=2 * weight.size, transcendentals=0
        ),
    )(*parts, weight)


def project_near(attended, weight):
    whole = jax.ShapeDtypeStruct((ROWS, weight.shape[1] // 5), jnp.bfloat16)
    return pl.pallas_call(
        near_kernel,
        out_shape=(whole,) * 5,
        in_specs=[VMEM] * 2,
        out_specs=(VMEM,) * 5,
        compiler_params=pltpu.CompilerParams(vmem_limit_bytes=24 * 1024 * 1024),
        cost_estimate=pl.CostEstimate(
            flops=2 * ROWS * weight.size, bytes_accessed=2 * weight.size, transcendentals=0
        ),
    )(attended, weight)


def sum_over_hd(far, near):
    ahead3, behind3, ahead4, behind4 = far
    ahead2, behind2, ahead1, behind1, here = near

    def move(rows, step):
        return lax.ppermute(rows, "hd", [(i, (i + step) % NY) for i in range(NY)])

    def wide(rows):
        return rows.astype(jnp.float32)

    half = ahead4.shape[1]
    from3, from_far3 = move(ahead3, 1), move(behind3, -1)
    from4, from_far4 = move(ahead4, 2), move(behind4, -2)
    onward = wide(ahead2) + wide(from3) + jnp.pad(wide(from4), ((0, 0), (0, half)))
    backward = wide(behind2) + wide(from_far3) + jnp.pad(wide(from_far4), ((0, 0), (half, 0)))
    from2 = move(onward.astype(jnp.bfloat16), 2)
    from_far2 = move(backward.astype(jnp.bfloat16), -2)
    from1, from_far1 = move(ahead1, 1), move(behind1, -1)
    total = wide(here) + wide(from1) + wide(from_far1) + wide(from2) + wide(from_far2)
    return total.astype(jnp.bfloat16)


def per_device(query_rows, key_rows, value_rows, doc_ids, out_weight):
    place = lax.axis_index("ctx").reshape(1)

    def id_rows(columns):
        return jnp.pad(doc_ids[None, :], ((0, PAD - 1), (0, columns - 4))).astype(jnp.bfloat16)

    q_packed = jnp.concatenate([query_rows, id_rows(query_rows.shape[1])], axis=0)
    q_blocks = [q_packed] + [
        lax.ppermute(q_packed, "ctx", ctx_perm(lambda z, x, c, r=r: (z, x + r, c)))
        for r in range(1, NX)
    ]
    kv_packed = jnp.concatenate([key_rows, value_rows, id_rows(HDIM)], axis=0)
    kv_own = lax.all_to_all(
        jnp.broadcast_to(kv_packed[None], (NZ,) + kv_packed.shape),
        "ctx",
        0,
        0,
        axis_index_groups=Z_GROUPS,
    )
    y = lax.axis_index("hd")
    *q_blocks, kv_own = lax.optimization_barrier((*q_blocks, kv_own))
    kv_other = lax.ppermute(kv_own, "ctx", ctx_perm(lambda z, x, c: (z, x, 1 - c)))

    q_ids = jnp.stack([block[ROWS, 0:4] for block in q_blocks]).astype(jnp.int32)
    own_ids = kv_own[:, 2 * ROWS, 0:4].astype(jnp.int32)
    other_ids = kv_other[:, 2 * ROWS, 0:4].astype(jnp.int32)
    k_held, v_turned = hold(place, kv_own, kv_other)
    arrays = (place, q_ids, own_ids, other_ids, q_blocks, k_held, v_turned)
    made = dict(zip(FOREIGN, attend(FOREIGN, *arrays)))
    made[2], weight = lax.optimization_barrier((made[2], out_weight))
    parts = {
        r: lax.ppermute(made[r], "ctx", ctx_perm(lambda z, x, c, r=r: (z, x - r, c)))
        for r in FOREIGN
    }
    (parts[0],) = attend((0,), *arrays)
    far_weight = columns_of(y, weight, (3, -3, 4))
    near_weight = columns_of(y, weight, (2, -2, 1, -1, 0))
    attended, kept, *far = project_far([parts[r] for r in (0, 2, 1, 3)], far_weight)
    near = project_near(kept, near_weight)
    return attended, sum_over_hd(far, near)


def solution(mesh):
    in_specs = (P("ctx", "hd"), P("ctx", "hd"), P("ctx", "hd"), P("ctx"), P("hd", None))
    out_specs = (P("ctx", "hd"), P("ctx", "hd"))
    return jax.shard_map(
        per_device, mesh=mesh, in_specs=in_specs, out_specs=out_specs, check_vma=False
    )
```
